512 devices in a mesh: dp: 16 (over x_hi, y, core), expert: 32 (over x_lo, z).
Axes of the slice: x: 4 (x_hi: 2, x_lo: 2; x = x_hi * 2 + x_lo), y: 4, z: 16, core: 2. Of those that a mesh axis runs over, the one named last changes fastest.
Arguments:
- tokens: bfloat16 [65536, 1024], P(('dp', 'expert')), may hold values from -6 to 6
- cotangent: bfloat16 [65536, 1024], P(('dp', 'expert')), may hold values from -6 to 6
- picks: int32 [512, 64], P(('dp', 'expert')), may hold values from 0 to 127
- gates: float32 [512, 64], P(('dp', 'expert')), may hold values from 0.1 to 1
- w_gate: bfloat16 [64, 2816, 1024], P('expert', 'dp'), may hold values from -0.1875 to 0.1875
- w_up: bfloat16 [64, 2816, 1024], P('expert', 'dp'), may hold values from -0.1875 to 0.1875
- w_down: bfloat16 [64, 2816, 1024], P('expert', 'dp'), may hold values from -0.109375 to 0.109375
Outputs:
- grad_tokens: bfloat16 [65536, 1024], P(('dp', 'expert'))
- grad_gate: bfloat16 [64, 2816, 1024], P('expert', 'dp')
- grad_up: bfloat16 [64, 2816, 1024], P('expert', 'dp')
- grad_down: bfloat16 [64, 2816, 1024], P('expert', 'dp')
The draws below stay inside these ranges and needn't reach their ends.
Inputs may be any that keep to these rules, and one draw needn't show every extreme that they name: picks[s, e] is the row, among the 128 tokens of device s, that expert e takes from device s.
All inputs are finite; a program needn't handle non-finite values.
Results may differ from the reference program's by a relative error of at most 0.02.
Values may be sent and summed in bfloat16 or wider, within the bound.
No kernel may reach another device: no remote copies, remote signals or barrier semaphores. Data moves between devices by JAX's collectives and lax.ppermute only.
A program may use at most 64 MiB of HBM per device.

```python
import math
import jax
import jax.numpy as jnp
from jax import lax

D = 1024
F = 2816
TOK_DEV = 128
E = 64
SOURCES = 512
TOKENS = 65536
N_DP = 16


def place_ends(values, rng, least, largest):
    spot = [jax.random.randint(jax.random.fold_in(rng, axis), (), 0, length) for axis, length in enumerate(values.shape)]
    widest = values.shape.index(max(values.shape))
    beside = spot[:widest] + [(spot[widest] + 1) % values.shape[widest]] + spot[widest + 1:]
    return values.at[tuple(spot)].set(least).at[tuple(beside)].set(largest)


def block_scale(key, shape, cuts, low, high):
    level, own = 1.0, jax.random.fold_in(key, 6)
    for axis_at, blocks in cuts:
        heights = jnp.exp(jax.random.uniform(jax.random.fold_in(own, axis_at), (blocks,), jnp.float32, low / len(cuts), high / len(cuts)))
        level = level * jnp.repeat(heights, shape[axis_at] // blocks).reshape([-1 if axis == axis_at else 1 for axis in range(len(shape))])
    return level


def normal_values(stream_key, extent, spread, bound, shards=(), kind=jnp.bfloat16):
    entries = spread * jax.random.normal(stream_key, extent, jnp.float32)
    if shards:
        entries = entries * block_scale(stream_key, extent, shards, -0.22, 0.18)
    return jnp.clip(entries, -bound, bound).astype(kind)


def setup_inputs(seed: int = 0) -> dict:
    key_list = jax.random.split(jax.random.key(seed), 8)
    return {
        "tokens": normal_values(key_list[0], (TOKENS, D), 1.0, 6.0, ((0, 512),)),
        "cotangent": normal_values(key_list[1], (TOKENS, D), 1.0, 6.0, ((0, 512),)),
        "picks": place_ends(jax.random.randint(key_list[2], (SOURCES, E), 0, TOK_DEV), jax.random.fold_in(key_list[2], 1), 0, TOK_DEV - 1).astype(jnp.int32),
        "gates": jnp.clip(jnp.exp(math.log(1.0) - 2.3025851 * jax.random.uniform(key_list[3], (SOURCES, E), jnp.float32) ** block_scale(key_list[3], (SOURCES, E), ((0, 512),), -0.2, 0.2)), 0.1, 1.0),
        "w_gate": normal_values(key_list[4], (E, F, D), D ** -0.5, 0.1875, ((0, 32), (1, 16))),
        "w_up": normal_values(key_list[5], (E, F, D), D ** -0.5, 0.1875, ((0, 32), (1, 16))),
        "w_down": normal_values(key_list[6], (E, F, D), F ** -0.5, 0.109375, ((0, 32), (1, 16))),
    }


def reference(tokens, cotangent, picks, gates, w_gate, w_up, w_down):
    base = (jnp.arange(SOURCES, dtype=jnp.int32) * TOK_DEV)[:, None]
    indices = (picks + base).astype(jnp.int32).T
    weights_t = gates.T
    block = F // N_DP

    def expert(args):
        rows_idx, gate_col, wg, wu, wd = args
        inputs = tokens[rows_idx]
        scaled = (cotangent[rows_idx].astype(jnp.float32) * gate_col[:, None]).astype(jnp.bfloat16)
        pre_gate = jnp.dot(inputs, wg.T, preferred_element_type=jnp.float32)
        pre_up = jnp.dot(inputs, wu.T, preferred_element_type=jnp.float32)
        sigmoid_g = jax.nn.sigmoid(pre_gate)
        active = pre_gate * sigmoid_g
        hidden = (active * pre_up).astype(jnp.bfloat16)
        grad_hidden = jnp.dot(scaled, wd.T, preferred_element_type=jnp.float32)
        g_down = jnp.dot(hidden.T, scaled, preferred_element_type=jnp.float32).astype(jnp.bfloat16)
        d_up = (grad_hidden * active).astype(jnp.bfloat16)
        d_gate = (grad_hidden * pre_up * sigmoid_g * (1.0 + pre_gate * (1.0 - sigmoid_g))).astype(jnp.bfloat16)
        g_gate = jnp.dot(d_gate.T, inputs, preferred_element_type=jnp.float32).astype(jnp.bfloat16)
        g_up = jnp.dot(d_up.T, inputs, preferred_element_type=jnp.float32).astype(jnp.bfloat16)
        dg_blocks = d_gate.astype(jnp.float32).reshape(SOURCES, N_DP, block)
        du_blocks = d_up.astype(jnp.float32).reshape(SOURCES, N_DP, block)
        wg_blocks = wg.astype(jnp.float32).reshape(N_DP, block, D)
        wu_blocks = wu.astype(jnp.float32).reshape(N_DP, block, D)
        parts = jnp.einsum("snf,nfd->snd", dg_blocks, wg_blocks) + jnp.einsum("snf,nfd->snd", du_blocks, wu_blocks)
        rows = jnp.sum(parts.astype(jnp.bfloat16).astype(jnp.float32), axis=1)
        return g_gate, g_up, g_down, rows

    grad_gate, grad_up, grad_down, all_rows = lax.map(expert, (indices, weights_t, w_gate, w_up, w_down))
    flat_idx = indices.reshape(-1)
    total = jnp.zeros((TOKENS, D), jnp.float32).at[flat_idx].add(all_rows.reshape(-1, D))
    return total.astype(jnp.bfloat16), grad_gate, grad_up, grad_down
```

```python
import jax
import jax.numpy as jnp
from jax import lax
from jax.sharding import Mesh, PartitionSpec as P

AXES = ("xh", "y", "core", "xl", "z")
DEST = ("xl", "z")
BATCH = ("xh", "y")
SWAP = ((0, 1), (1, 0))


def one_hot(rows, count):
    return (rows[:, None] == jnp.arange(count, dtype=jnp.int32)[None, :]).astype(jnp.bfloat16)


def shards(tokens, cotangent, picks, gates, w_gate, w_up, w_down):
    f32, bf16 = jnp.float32, jnp.bfloat16
    token_rows, width = tokens.shape
    groups = lax.axis_size(DEST)
    batches = lax.axis_size(BATCH)
    core = lax.axis_index("core")

    def pair(two):
        return jnp.where(core == 0, two[0], two[1]), jnp.where(core == 0, two[1], two[0])

    own, other = [], []
    for w in (w_gate, w_up, w_down):
        own.append(lax.dynamic_index_in_dim(w, core, 0, keepdims=False))
        other.append(lax.dynamic_index_in_dim(w, 1 - core, 0, keepdims=False))
    got_w = lax.ppermute(jnp.stack(other), "core", SWAP)
    wg, wu, wd = (jnp.concatenate([a, got_w[i]], 0) for i, a in enumerate(own))

    chosen = picks[0].reshape(groups, 2)
    weight = gates[0].reshape(groups, 2)
    keep_row, send_row = pair((chosen[:, 0], chosen[:, 1]))
    keep_gate, send_gate = pair((weight[:, 0], weight[:, 1]))
    order = jnp.concatenate([keep_row, send_row])
    scale = jnp.concatenate([keep_gate, send_gate])
    selector = one_hot(order, token_rows)
    x = jnp.dot(selector, tokens, preferred_element_type=f32).astype(bf16)
    dy = (jnp.dot(selector, cotangent, preferred_element_type=f32) * scale[:, None]).astype(bf16)
    x, dy = x.reshape(2, groups, width), dy.reshape(2, groups, width)
    got = lax.ppermute(jnp.stack([x[1], dy[1]]), "core", SWAP)
    out = jnp.stack([x[0], got[0], dy[0], got[1]], 1)
    rows = lax.all_to_all(out, DEST, split_axis=0, concat_axis=0, tiled=True)
    rows = rows.reshape(groups, 2, 2, width).transpose(1, 0, 2, 3).reshape(2, groups * 2, width)
    everyone = jnp.broadcast_to(rows[None], (batches, 2, groups * 2, width))
    gathered = lax.all_to_all(everyone, BATCH, split_axis=0, concat_axis=0, tiled=True)
    all_x = gathered[:, 0].reshape(-1, width)
    all_dy = gathered[:, 1].reshape(-1, width)

    def nt(a, b):
        return lax.dot_general(a, b, (((1,), (1,)), ((), ())), preferred_element_type=f32)

    def tn(a, b):
        return lax.dot_general(a, b, (((0,), (0,)), ((), ())), preferred_element_type=f32)

    pre_gate = nt(all_x, wg)
    pre_up = nt(all_x, wu)
    grad_hidden = nt(all_dy, wd)
    sig = jax.nn.sigmoid(pre_gate)
    active = pre_gate * sig
    hidden = (active * pre_up).astype(bf16)
    d_up = (grad_hidden * active).astype(bf16)
    d_gate = (grad_hidden * pre_up * sig * (1.0 + pre_gate * (1.0 - sig))).astype(bf16)
    part = (
        jnp.dot(d_gate, wg, preferred_element_type=f32)
        + jnp.dot(d_up, wu, preferred_element_type=f32)
    ).astype(bf16)
    parts = lax.all_to_all(
        part.reshape(batches, groups * 2, width), BATCH, split_axis=0, concat_axis=0, tiled=True
    )
    summed = jnp.sum(parts.astype(f32), 0).astype(bf16)

    grads = jnp.stack([tn(d_gate, all_x), tn(d_up, all_x), tn(hidden, all_dy)]).astype(bf16)
    half = grads.shape[1] // 2
    mine = grads[:, :half]
    theirs = lax.ppermute(grads[:, half:], "core", SWAP)
    first = jnp.where(core == 0, mine, theirs)
    second = jnp.where(core == 0, theirs, mine)
    grads = jnp.stack([first, second], 1)

    back = lax.all_to_all(
        summed.reshape(groups, 2, width), DEST, split_axis=0, concat_axis=0, tiled=True
    )
    away = lax.ppermute(back[:, 1], "core", SWAP)
    returned = jnp.concatenate([back[:, 0], away], 0)
    grad_tokens = lax.dot_general(
        selector, returned, (((0,), (0,)), ((), ())), preferred_element_type=f32
    ).astype(bf16)
    return grad_tokens, grads[0], grads[1], grads[2]


def solution(mesh):
    fine = Mesh(mesh.devices.reshape(2, 4, 2, 2, 16), AXES)
    rows = P(AXES, None)
    weights = P(DEST, ("xh", "y", "core"), None)
    return jax.shard_map(
        shards,
        mesh=fine,
        in_specs=(rows, rows, rows, rows, weights, weights, weights),
        out_specs=(rows, weights, weights, weights),
        check_vma=False,
    )
```

```python
import jax
import jax.numpy as jnp
from jax import lax
from jax.experimental import pallas as pl
from jax.experimental.pallas import tpu as pltpu
from jax.sharding import Mesh, PartitionSpec as P

AXES = ("xh", "y", "core", "xl", "z")
DEST = ("core", "xl", "z")
BATCH = ("xh", "y")
SWAP = ((0, 1), (1, 0))
F32, BF16 = jnp.float32, jnp.bfloat16


def iota(shape, axis):
    return lax.broadcasted_iota(jnp.int32, shape, axis)


def column(row, rows_each):
    count = row.shape[1]
    shape = (count * rows_each, count)
    place = iota(shape, 0) // rows_each
    expert = (place % (count // 2)) * 2 + place // (count // 2)
    spread = jnp.where(iota(shape, 1) == expert, jnp.broadcast_to(row, shape), 0.0)
    return jnp.sum(spread, axis=1, keepdims=True)


def pick_kernel(picks_in, gates_in, tokens_in, cotangent_in, out, picks, gates, both, sems):
    token_rows = tokens_in.shape[0]
    copies = [
        pltpu.make_async_copy(source, target, sems.at[i])
        for i, (source, target) in enumerate(
            (
                (picks_in, picks),
                (gates_in, gates),
                (tokens_in, both.at[pl.ds(0, token_rows)]),
                (cotangent_in, both.at[pl.ds(token_rows, token_rows)]),
            )
        )
    ]
    for copy in copies:
        copy.start()
    copies[0].wait()
    copies[1].wait()
    count = picks.shape[1]
    row = column(picks[...].astype(F32), 2).astype(jnp.int32)
    gate = column(gates[...], 2)
    shape = (2 * count, 2 * token_rows)
    odd = iota((2 * count, 1), 0) % 2
    selector = (iota(shape, 1) == row + odd * token_rows).astype(F32).astype(BF16)
    copies[2].wait()
    copies[3].wait()
    picked = jnp.dot(selector, both[...], preferred_element_type=F32)
    scaled = picked * jnp.where(odd == 1, gate, 1.0)
    out[...] = scaled.reshape(out.shape).astype(BF16)


def spread_kernel(rows, out, both, sems):
    count, width = both.shape[1:]
    for i in range(2):
        half = rows[:, 8 * i : 8 * i + 8, :].astype(F32)
        both[i] = half.reshape(count, width).astype(BF16)
    copies = [
        pltpu.make_async_copy(both, out.at[i], sems.at[i]) for i in range(out.shape[0])
    ]
    for copy in copies:
        copy.start()
    for copy in copies:
        copy.wait()


def sum_kernel(parts, out):
    out[...] = jnp.sum(parts[...].astype(F32), 0).astype(BF16)


def scatter_kernel(picks, returned, out):
    count, token_rows = picks.shape[1], out.shape[0]
    row = column(picks[...].astype(F32), 1).astype(jnp.int32)
    selector = (iota((count, token_rows), 1) == row).astype(F32).astype(BF16)
    out[...] = tn(selector, returned[...]).astype(BF16)


def fill_kernel(core_ref, *refs):
    away = 1 - core_ref[0]
    theirs, outs, sems = refs[:3], refs[6:9], refs[9]
    copies = [
        pltpu.make_async_copy(theirs[i].at[away], outs[i].at[away], sems.at[i]) for i in range(3)
    ]
    for copy in copies:
        copy.start()
    for copy in copies:
        copy.wait()


def nt(a, b):
    return lax.dot_general(a, b, (((1,), (1,)), ((), ())), preferred_element_type=F32)


def tn(a, b):
    return lax.dot_general(a, b, (((0,), (0,)), ((), ())), preferred_element_type=F32)


def products_kernel(got, own, other, down, part, acts):
    batches, _, count, width = got.shape
    x = got[:, 0].reshape(batches * count, width)
    dy = got[:, 1].reshape(batches * count, width)
    for half, gate_up in ((0, own), (1, other)):
        pre_gate = nt(gate_up[0], x)
        pre_up = nt(gate_up[1], x)
        grad_hidden = nt(down[half], dy)
        sig = jax.nn.sigmoid(pre_gate)
        active = pre_gate * sig
        acts[0, half] = (grad_hidden * pre_up * sig * (1.0 + pre_gate * (1.0 - sig))).astype(BF16)
        acts[1, half] = (grad_hidden * active).astype(BF16)
        acts[2, half] = (active * pre_up).astype(BF16)
    total = tn(acts[0, 0], own[0]) + tn(acts[1, 0], own[1])
    total += tn(acts[0, 1], other[0]) + tn(acts[1, 1], other[1])
    part[...] = total.astype(BF16).reshape(part.shape)


def grads_kernel(core_ref, acts, got, gate, up, down, *rest):
    sends, mine, sems = rest[:3], rest[3], rest[4]
    core = core_ref[0]
    rows = got.shape[0] * got.shape[2]
    stores = []
    for i, out in enumerate((gate, up, down)):
        side = got[:, i // 2].reshape(rows, got.shape[3])
        mine[i] = jnp.dot(acts[i, 0], side, preferred_element_type=F32).astype(BF16)
        stores.append(pltpu.make_async_copy(mine.at[i], out.at[core], sems.at[i]))
        stores[-1].start()
        sends[i][...] = jnp.dot(acts[i, 1], side, preferred_element_type=F32).astype(BF16)
    for copy in stores:
        copy.wait()


def shards(tokens, cotangent, picks, gates, w_gate, w_up, w_down):
    token_rows, width = tokens.shape
    count = picks.shape[1]
    units = w_gate.shape[1]
    core = lax.axis_index("core")
    small = pltpu.CompilerParams(vmem_limit_bytes=12 * 2**20)
    full = pltpu.CompilerParams(vmem_limit_bytes=63 * 2**20)
    medium = pltpu.CompilerParams(vmem_limit_bytes=20 * 2**20)
    scalar = pl.BlockSpec(memory_space=pltpu.SMEM)
    near = pl.BlockSpec(memory_space=pltpu.VMEM)
    far = pl.BlockSpec(memory_space=pl.ANY)
    place = core.reshape(1)

    def of(expert, *arrays):
        return jnp.stack(
            [lax.dynamic_index_in_dim(w, expert, 0, keepdims=False) for w in arrays]
        )

    own = of(core, w_gate, w_up)
    other = lax.ppermute(of(1 - core, w_gate, w_up), "core", SWAP)
    down = jnp.concatenate(
        [of(core, w_down), lax.ppermute(of(1 - core, w_down), "core", SWAP)], 0
    )

    out = pl.pallas_call(
        pick_kernel,
        in_specs=[far] * 4,
        out_specs=near,
        out_shape=jax.ShapeDtypeStruct((count, 16, width // 8), BF16),
        scratch_shapes=[
            pltpu.VMEM((1, count), jnp.int32),
            pltpu.VMEM((1, count), F32),
            pltpu.VMEM((2 * token_rows, width), BF16),
            pltpu.SemaphoreType.DMA((4,)),
        ],
        compiler_params=full,
    )(picks, gates, tokens, cotangent)
    rows = lax.all_to_all(out, DEST, split_axis=0, concat_axis=0, tiled=True)
    batches = lax.axis_size(BATCH)
    sources = batches * count
    everyone = pl.pallas_call(
        spread_kernel,
        in_specs=[near],
        out_specs=far,
        out_shape=jax.ShapeDtypeStruct((batches, 2, count, width), BF16),
        scratch_shapes=[
            pltpu.VMEM((2, count, width), BF16),
            pltpu.SemaphoreType.DMA((batches,)),
        ],
        compiler_params=full,
    )(rows)
    got = lax.all_to_all(everyone, BATCH, split_axis=0, concat_axis=0, tiled=True)

    part, acts = pl.pallas_call(
        products_kernel,
        in_specs=[near] * 4,
        out_specs=[near] * 2,
        out_shape=[
            jax.ShapeDtypeStruct((batches, count, width), BF16),
            jax.ShapeDtypeStruct((3, 2, units, sources), BF16),
        ],
        cost_estimate=pl.CostEstimate(
            flops=20 * sources * units * width, bytes_accessed=8 * 2**20, transcendentals=0
        ),
        compiler_params=medium,
    )(got, own, other, down)
    parts = lax.all_to_all(part, BATCH, split_axis=0, concat_axis=0, tiled=True)

    side = jax.ShapeDtypeStruct((units, width), BF16)
    grad = jax.ShapeDtypeStruct((2, units, width), BF16)
    results = pl.pallas_call(
        grads_kernel,
        in_specs=[scalar, near, near],
        out_specs=[far] * 3 + [near] * 3,
        out_shape=[grad] * 3 + [side] * 3,
        scratch_shapes=[pltpu.VMEM((3, units, width), BF16), pltpu.SemaphoreType.DMA((3,))],
        cost_estimate=pl.CostEstimate(
            flops=12 * sources * units * width, bytes_accessed=6 * 2**20, transcendentals=0
        ),
        compiler_params=medium,
    )(place, acts, got)
    theirs = [lax.all_gather(send, "core", axis=0) for send in results[3:]]
    grads = pl.pallas_call(
        fill_kernel,
        in_specs=[scalar] + [near] * 3 + [far] * 3,
        out_specs=[far] * 3,
        out_shape=[grad] * 3,
        input_output_aliases={4: 0, 5: 1, 6: 2},
        scratch_shapes=[pltpu.SemaphoreType.DMA((3,))],
        compiler_params=small,
    )(place, *theirs, *results[:3])
    summed = pl.pallas_call(
        sum_kernel,
        in_specs=[near],
        out_specs=near,
        out_shape=jax.ShapeDtypeStruct((count, width), BF16),
        compiler_params=small,
    )(parts)
    returned = lax.all_to_all(
        summed.reshape(count, 2, width // 2), DEST, split_axis=0, concat_axis=0, tiled=True
    )
    grad_tokens = pl.pallas_call(
        scatter_kernel,
        in_specs=[near, near],
        out_specs=near,
        out_shape=jax.ShapeDtypeStruct((token_rows, width), BF16),
        compiler_params=small,
    )(picks, returned.reshape(count, width))
    return grad_tokens, *grads


def solution(mesh):
    fine = Mesh(mesh.devices.reshape(2, 4, 2, 2, 16), AXES)
    rows = P(AXES, None)
    weights = P(("xl", "z"), ("xh", "y", "core"), None)
    return jax.shard_map(
        shards,
        mesh=fine,
        in_specs=(rows, rows, rows, rows, weights, weights, weights),
        out_specs=(rows, weights, weights, weights),
        check_vma=False,
    )
```

```python
import jax
import jax.numpy as jnp
from jax import lax
from jax.experimental import pallas as pl
from jax.experimental.pallas import tpu as pltpu
from jax.sharding import Mesh, PartitionSpec as P

AXES = ("xh", "y", "core", "xl", "z")
DEST = ("core", "xl", "z")
BATCH = ("xh", "y")
SWAP = ((0, 1), (1, 0))
F32, BF16 = jnp.float32, jnp.bfloat16


def iota(shape, axis):
    return lax.broadcasted_iota(jnp.int32, shape, axis)


def column(row, rows_each):
    count = row.shape[1]
    shape = (count * rows_each, count)
    place = iota(shape, 0) // rows_each
    expert = (place % (count // 2)) * 2 + place // (count // 2)
    spread = jnp.where(iota(shape, 1) == expert, jnp.broadcast_to(row, shape), 0.0)
    return jnp.sum(spread, axis=1, keepdims=True)


def pick_kernel(picks_in, gates_in, tokens_in, cotangent_in, out, picks, gates, both, sems):
    token_rows = tokens_in.shape[0]
    copies = [
        pltpu.make_async_copy(source, target, sems.at[i])
        for i, (source, target) in enumerate(
            (
                (picks_in, picks),
                (gates_in, gates),
                (tokens_in, both.at[pl.ds(0, token_rows)]),
                (cotangent_in, both.at[pl.ds(token_rows, token_rows)]),
            )
        )
    ]
    for copy in copies:
        copy.start()
    copies[0].wait()
    copies[1].wait()
    count = picks.shape[1]
    row = column(picks[...].astype(F32), 2).astype(jnp.int32)
    gate = column(gates[...], 2)
    shape = (2 * count, 2 * token_rows)
    odd = iota((2 * count, 1), 0) % 2
    selector = (iota(shape, 1) == row + odd * token_rows).astype(F32).astype(BF16)
    copies[2].wait()
    copies[3].wait()
    picked = jnp.dot(selector, both[...], preferred_element_type=F32)
    scaled = picked * jnp.where(odd == 1, gate, 1.0)
    out[...] = scaled.reshape(out.shape).astype(BF16)


def spread_kernel(rows, out, both, sems):
    count, width = both.shape[1:]
    values = rows[...].astype(F32)
    copies = []
    for kind in range(2):
        half = values[:, 8 * kind : 8 * kind + 8, :]
        both[kind] = half.reshape(count, width).astype(BF16)
        for i in range(out.shape[0]):
            copies.append(
                pltpu.make_async_copy(both.at[kind], out.at[i, kind], sems.at[kind, i])
            )
            copies[-1].start()
    for copy in copies:
        copy.wait()


def sum_kernel(parts, filled, out):
    out[...] = jnp.sum(parts[...].astype(F32), 0).astype(BF16)


def scatter_kernel(picks, returned, out):
    count, token_rows = picks.shape[1], out.shape[0]
    row = column(picks[...].astype(F32), 1).astype(jnp.int32)
    selector = (iota((count, token_rows), 1) == row).astype(F32).astype(BF16)
    out[...] = tn(selector, returned[...]).astype(BF16)


def fill_kernel(core_ref, *refs):
    away = 1 - core_ref[0]
    theirs, (filled, *outs), sems = refs[:3], refs[6:10], refs[10]
    copies = [
        pltpu.make_async_copy(theirs[i].at[away], outs[i].at[away], sems.at[i]) for i in range(3)
    ]
    for copy in copies:
        copy.start()
    for copy in copies:
        copy.wait()
    filled[...] = jnp.ones_like(filled)


def nt(a, b):
    return lax.dot_general(a, b, (((1,), (1,)), ((), ())), preferred_element_type=F32)


def tn(a, b):
    return lax.dot_general(a, b, (((0,), (0,)), ((), ())), preferred_element_type=F32)


def products_kernel(got, own, other, down, part, acts):
    batches, _, count, width = got.shape
    x = got[:, 0].reshape(batches * count, width)
    dy = got[:, 1].reshape(batches * count, width)
    for half, gate_up in ((0, own), (1, other)):
        pre_gate = nt(gate_up[0], x)
        pre_up = nt(gate_up[1], x)
        grad_hidden = nt(down[half], dy)
        sig = jax.nn.sigmoid(pre_gate)
        active = pre_gate * sig
        acts[0, half] = (grad_hidden * pre_up * sig * (1.0 + pre_gate * (1.0 - sig))).astype(BF16)
        acts[1, half] = (grad_hidden * active).astype(BF16)
        acts[2, half] = (active * pre_up).astype(BF16)
    total = tn(acts[0, 0], own[0]) + tn(acts[1, 0], own[1])
    total += tn(acts[0, 1], other[0]) + tn(acts[1, 1], other[1])
    part[...] = total.astype(BF16).reshape(part.shape)


def grads_kernel(core_ref, acts, got, gate, up, down, *rest):
    sends, mine, sems = rest[:3], rest[3], rest[4]
    core = core_ref[0]
    rows = got.shape[0] * got.shape[2]
    stores = []
    for i, out in enumerate((gate, up, down)):
        side = got[:, i // 2].reshape(rows, got.shape[3])
        mine[i] = jnp.dot(acts[i, 0], side, preferred_element_type=F32).astype(BF16)
        stores.append(pltpu.make_async_copy(mine.at[i], out.at[core], sems.at[i]))
        stores[-1].start()
        sends[i][...] = jnp.dot(acts[i, 1], side, preferred_element_type=F32).astype(BF16)
    for copy in stores:
        copy.wait()


def shards(tokens, cotangent, picks, gates, w_gate, w_up, w_down):
    token_rows, width = tokens.shape
    count = picks.shape[1]
    units = w_gate.shape[1]
    core = lax.axis_index("core")
    small = pltpu.CompilerParams(vmem_limit_bytes=12 * 2**20)
    full = pltpu.CompilerParams(vmem_limit_bytes=63 * 2**20)
    medium = pltpu.CompilerParams(vmem_limit_bytes=20 * 2**20)
    scalar = pl.BlockSpec(memory_space=pltpu.SMEM)
    near = pl.BlockSpec(memory_space=pltpu.VMEM)
    far = pl.BlockSpec(memory_space=pl.ANY)
    place = core.reshape(1)

    def of(expert, *arrays):
        return jnp.stack(
            [lax.dynamic_index_in_dim(w, expert, 0, keepdims=False) for w in arrays]
        )

    own = of(core, w_gate, w_up)
    other = lax.ppermute(of(1 - core, w_gate, w_up), "core", SWAP)
    down = jnp.concatenate(
        [of(core, w_down), lax.ppermute(of(1 - core, w_down), "core", SWAP)], 0
    )

    out = pl.pallas_call(
        pick_kernel,
        in_specs=[far] * 4,
        out_specs=near,
        out_shape=jax.ShapeDtypeStruct((count, 16, width // 8), BF16),
        scratch_shapes=[
            pltpu.VMEM((1, count), jnp.int32),
            pltpu.VMEM((1, count), F32),
            pltpu.VMEM((2 * token_rows, width), BF16),
            pltpu.SemaphoreType.DMA((4,)),
        ],
        compiler_params=full,
    )(picks, gates, tokens, cotangent)
    rows = lax.all_to_all(out, DEST, split_axis=0, concat_axis=0, tiled=True)
    batches = lax.axis_size(BATCH)
    sources = batches * count
    everyone = pl.pallas_call(
        spread_kernel,
        in_specs=[near],
        out_specs=far,
        out_shape=jax.ShapeDtypeStruct((batches, 2, count, width), BF16),
        scratch_shapes=[
            pltpu.VMEM((2, count, width), BF16),
            pltpu.SemaphoreType.DMA((2, batches)),
        ],
        compiler_params=full,
    )(rows)
    got = lax.all_to_all(everyone, BATCH, split_axis=0, concat_axis=0, tiled=True)

    part, acts = pl.pallas_call(
        products_kernel,
        in_specs=[near] * 4,
        out_specs=[near] * 2,
        out_shape=[
            jax.ShapeDtypeStruct((batches, count, width), BF16),
            jax.ShapeDtypeStruct((3, 2, units, sources), BF16),
        ],
        cost_estimate=pl.CostEstimate(
            flops=20 * sources * units * width, bytes_accessed=8 * 2**20, transcendentals=0
        ),
        compiler_params=medium,
    )(got, own, other, down)
    parts = lax.all_to_all(part, BATCH, split_axis=0, concat_axis=0, tiled=True)

    side = jax.ShapeDtypeStruct((units, width), BF16)
    grad = jax.ShapeDtypeStruct((2, units, width), BF16)
    results = pl.pallas_call(
        grads_kernel,
        in_specs=[scalar, near, near],
        out_specs=[far] * 3 + [near] * 3,
        out_shape=[grad] * 3 + [side] * 3,
        scratch_shapes=[pltpu.VMEM((3, units, width), BF16), pltpu.SemaphoreType.DMA((3,))],
        cost_estimate=pl.CostEstimate(
            flops=12 * sources * units * width, bytes_accessed=6 * 2**20, transcendentals=0
        ),
        compiler_params=medium,
    )(place, acts, got)
    theirs = [lax.all_gather(send, "core", axis=0) for send in results[3:]]
    filled, *grads = pl.pallas_call(
        fill_kernel,
        in_specs=[scalar] + [near] * 3 + [far] * 3,
        out_specs=[near] + [far] * 3,
        out_shape=[jax.ShapeDtypeStruct((8, 128), F32)] + [grad] * 3,
        input_output_aliases={4: 1, 5: 2, 6: 3},
        scratch_shapes=[pltpu.SemaphoreType.DMA((3,))],
        compiler_params=small,
    )(place, *theirs, *results[:3])
    summed = pl.pallas_call(
        sum_kernel,
        in_specs=[near] * 2,
        out_specs=near,
        out_shape=jax.ShapeDtypeStruct((count, width), BF16),
        compiler_params=small,
    )(parts, filled)
    returned = lax.all_to_all(
        summed.reshape(count, 2, width // 2), DEST, split_axis=0, concat_axis=0, tiled=True
    )
    grad_tokens = pl.pallas_call(
        scatter_kernel,
        in_specs=[near, near],
        out_specs=near,
        out_shape=jax.ShapeDtypeStruct((token_rows, width), BF16),
        compiler_params=small,
    )(picks, returned.reshape(count, width))
    return grad_tokens, *grads


def solution(mesh):
    fine = Mesh(mesh.devices.reshape(2, 4, 2, 2, 16), AXES)
    rows = P(AXES, None)
    weights = P(("xl", "z"), ("xh", "y", "core"), None)
    return jax.shard_map(
        shards,
        mesh=fine,
        in_specs=(rows, rows, rows, rows, weights, weights, weights),
        out_specs=(rows, weights, weights, weights),
        check_vma=False,
    )
```

```python
import jax
import jax.numpy as jnp
from jax import lax
from jax.experimental import pallas as pl
from jax.experimental.pallas import tpu as pltpu
from jax.sharding import Mesh, PartitionSpec as P

AXES = ("xh", "y", "core", "xl", "z")
DEST = ("core", "xl", "z")
BATCH = ("xh", "y")
SWAP = ((0, 1), (1, 0))
F32, BF16 = jnp.float32, jnp.bfloat16


def iota(shape, axis):
    return lax.broadcasted_iota(jnp.int32, shape, axis)


def column(row, rows_each):
    count = row.shape[1]
    shape = (count * rows_each, count)
    place = iota(shape, 0) // rows_each
    expert = (place % (count // 2)) * 2 + place // (count // 2)
    spread = jnp.where(iota(shape, 1) == expert, jnp.broadcast_to(row, shape), 0.0)
    return jnp.sum(spread, axis=1, keepdims=True)


def pick_kernel(picks_in, gates_in, tokens_in, cotangent_in, out, picks, gates, both, sems):
    token_rows = tokens_in.shape[0]
    copies = [
        pltpu.make_async_copy(source, target, sems.at[i])
        for i, (source, target) in enumerate(
            (
                (picks_in, picks),
                (gates_in, gates),
                (tokens_in, both.at[pl.ds(0, token_rows)]),
                (cotangent_in, both.at[pl.ds(token_rows, token_rows)]),
            )
        )
    ]
    for copy in copies:
        copy.start()
    copies[0].wait()
    copies[1].wait()
    count = picks.shape[1]
    row = column(picks[...].astype(F32), 2).astype(jnp.int32)
    gate = column(gates[...], 2)
    shape = (2 * count, 2 * token_rows)
    odd = iota((2 * count, 1), 0) % 2
    selector = (iota(shape, 1) == row + odd * token_rows).astype(F32).astype(BF16)
    copies[2].wait()
    copies[3].wait()
    picked = jnp.dot(selector, both[...], preferred_element_type=F32)
    scaled = picked * jnp.where(odd == 1, gate, 1.0)
    out[...] = scaled.reshape(out.shape).astype(BF16)


def spread_kernel(rows, weights, out):
    batches, _, count, width = out.shape
    values = rows[...].astype(F32)
    for kind in range(2):
        half = values[:, 8 * kind : 8 * kind + 8, :]
        half = half.reshape(count, width).astype(BF16)
        for i in range(batches):
            out[i, kind] = half


def sum_kernel(parts, filled, out):
    out[...] = jnp.sum(parts[...].astype(F32), 0).astype(BF16)


def scatter_kernel(picks, returned, out):
    count, token_rows = picks.shape[1], out.shape[0]
    row = column(picks[...].astype(F32), 1).astype(jnp.int32)
    selector = (iota((count, token_rows), 1) == row).astype(F32).astype(BF16)
    out[...] = tn(selector, returned[...]).astype(BF16)


def fill_kernel(core_ref, *refs):
    away = 1 - core_ref[0]
    theirs, (filled, *outs), sems = refs[:3], refs[6:10], refs[10]
    copies = [
        pltpu.make_async_copy(theirs[i].at[away], outs[i].at[away], sems.at[i]) for i in range(3)
    ]
    for copy in copies:
        copy.start()
    for copy in copies:
        copy.wait()
    filled[...] = jnp.ones_like(filled)


def nt(a, b):
    return lax.dot_general(a, b, (((1,), (1,)), ((), ())), preferred_element_type=F32)


def tn(a, b):
    return lax.dot_general(a, b, (((0,), (0,)), ((), ())), preferred_element_type=F32)


def products_kernel(got, weights, part, acts):
    batches, _, count, width = got.shape
    x = got[:, 0].reshape(batches * count, width)
    dy = got[:, 1].reshape(batches * count, width)
    for half in range(2):
        pre_gate = nt(weights[half, 0], x)
        pre_up = nt(weights[half, 1], x)
        grad_hidden = nt(weights[half, 2], dy)
        sig = jax.nn.sigmoid(pre_gate)
        active = pre_gate * sig
        acts[0, half] = (grad_hidden * pre_up * sig * (1.0 + pre_gate * (1.0 - sig))).astype(BF16)
        acts[1, half] = (grad_hidden * active).astype(BF16)
        acts[2, half] = (active * pre_up).astype(BF16)
    total = tn(acts[0, 0], weights[0, 0]) + tn(acts[1, 0], weights[0, 1])
    total += tn(acts[0, 1], weights[1, 0]) + tn(acts[1, 1], weights[1, 1])
    part[...] = total.astype(BF16).reshape(part.shape)


def grads_kernel(core_ref, acts, got, gate, up, down, *rest):
    sends, mine, sems = rest[:3], rest[3], rest[4]
    core = core_ref[0]
    rows = got.shape[0] * got.shape[2]
    stores = []
    for i, out in enumerate((gate, up, down)):
        side = got[:, i // 2].reshape(rows, got.shape[3])
        mine[i] = jnp.dot(acts[i, 0], side, preferred_element_type=F32).astype(BF16)
        stores.append(pltpu.make_async_copy(mine.at[i], out.at[core], sems.at[i]))
        stores[-1].start()
        sends[i][...] = jnp.dot(acts[i, 1], side, preferred_element_type=F32).astype(BF16)
    for copy in stores:
        copy.wait()


def shards(tokens, cotangent, picks, gates, w_gate, w_up, w_down):
    token_rows, width = tokens.shape
    count = picks.shape[1]
    units = w_gate.shape[1]
    core = lax.axis_index("core")
    small = pltpu.CompilerParams(vmem_limit_bytes=12 * 2**20)
    full = pltpu.CompilerParams(vmem_limit_bytes=63 * 2**20)
    medium = pltpu.CompilerParams(vmem_limit_bytes=20 * 2**20)
    scalar = pl.BlockSpec(memory_space=pltpu.SMEM)
    near = pl.BlockSpec(memory_space=pltpu.VMEM)
    far = pl.BlockSpec(memory_space=pl.ANY)
    place = core.reshape(1)

    def of(expert, *arrays):
        return jnp.stack(
            [lax.dynamic_index_in_dim(w, expert, 0, keepdims=False) for w in arrays]
        )

    halves = jnp.stack(
        [
            of(core, w_gate, w_up, w_down),
            jnp.concatenate(
                [
                    lax.ppermute(of(1 - core, *arrays), "core", SWAP)
                    for arrays in ((w_gate, w_up), (w_down,))
                ],
                0,
            ),
        ]
    )

    out = pl.pallas_call(
        pick_kernel,
        in_specs=[far] * 4,
        out_specs=near,
        out_shape=jax.ShapeDtypeStruct((count, 16, width // 8), BF16),
        scratch_shapes=[
            pltpu.VMEM((1, count), jnp.int32),
            pltpu.VMEM((1, count), F32),
            pltpu.VMEM((2 * token_rows, width), BF16),
            pltpu.SemaphoreType.DMA((4,)),
        ],
        compiler_params=full,
    )(picks, gates, tokens, cotangent)
    rows = lax.all_to_all(out, DEST, split_axis=0, concat_axis=0, tiled=True)
    batches = lax.axis_size(BATCH)
    sources = batches * count
    everyone = pl.pallas_call(
        spread_kernel,
        in_specs=[near, far],
        out_specs=near,
        out_shape=jax.ShapeDtypeStruct((batches, 2, count, width), BF16),
        compiler_params=small,
    )(rows, halves)
    got = lax.all_to_all(everyone, BATCH, split_axis=0, concat_axis=0, tiled=True)

    part, acts = pl.pallas_call(
        products_kernel,
        in_specs=[near] * 2,
        out_specs=[near] * 2,
        out_shape=[
            jax.ShapeDtypeStruct((batches, count, width), BF16),
            jax.ShapeDtypeStruct((3, 2, units, sources), BF16),
        ],
        cost_estimate=pl.CostEstimate(
            flops=20 * sources * units * width, bytes_accessed=8 * 2**20, transcendentals=0
        ),
        compiler_params=medium,
    )(got, halves)
    parts = lax.all_to_all(part, BATCH, split_axis=0, concat_axis=0, tiled=True)

    side = jax.ShapeDtypeStruct((units, width), BF16)
    grad = jax.ShapeDtypeStruct((2, units, width), BF16)
    results = pl.pallas_call(
        grads_kernel,
        in_specs=[scalar, near, near],
        out_specs=[far] * 3 + [near] * 3,
        out_shape=[grad] * 3 + [side] * 3,
        scratch_shapes=[pltpu.VMEM((3, units, width), BF16), pltpu.SemaphoreType.DMA((3,))],
        cost_estimate=pl.CostEstimate(
            flops=12 * sources * units * width, bytes_accessed=6 * 2**20, transcendentals=0
        ),
        compiler_params=medium,
    )(place, acts, got)
    theirs = [lax.all_gather(send, "core", axis=0) for send in results[3:]]
    filled, *grads = pl.pallas_call(
        fill_kernel,
        in_specs=[scalar] + [near] * 3 + [far] * 3,
        out_specs=[near] + [far] * 3,
        out_shape=[jax.ShapeDtypeStruct((8, 128), F32)] + [grad] * 3,
        input_output_aliases={4: 1, 5: 2, 6: 3},
        scratch_shapes=[pltpu.SemaphoreType.DMA((3,))],
        compiler_params=small,
    )(place, *theirs, *results[:3])
    summed = pl.pallas_call(
        sum_kernel,
        in_specs=[near] * 2,
        out_specs=near,
        out_shape=jax.ShapeDtypeStruct((count, width), BF16),
        compiler_params=small,
    )(parts, filled)
    returned = lax.all_to_all(
        summed.reshape(count, 2, width // 2), DEST, split_axis=0, concat_axis=0, tiled=True
    )
    grad_tokens = pl.pallas_call(
        scatter_kernel,
        in_specs=[near, near],
        out_specs=near,
        out_shape=jax.ShapeDtypeStruct((token_rows, width), BF16),
        compiler_params=small,
    )(picks, returned.reshape(count, width))
    return grad_tokens, *grads


def solution(mesh):
    fine = Mesh(mesh.devices.reshape(2, 4, 2, 2, 16), AXES)
    rows = P(AXES, None)
    weights = P(("xl", "z"), ("xh", "y", "core"), None)
    return jax.shard_map(
        shards,
        mesh=fine,
        in_specs=(rows, rows, rows, rows, weights, weights, weights),
        out_specs=(rows, weights, weights, weights),
        check_vma=False,
    )
```

```python
import jax
import jax.numpy as jnp
from jax import lax
from jax.experimental import pallas as pl
from jax.experimental.pallas import tpu as pltpu
from jax.sharding import Mesh, PartitionSpec as P

AXES = ("xh", "y", "core", "xl", "z")
DEST = ("core", "xl", "z")
BATCH = ("y", "xh")
SWAP = ((0, 1), (1, 0))
F32, BF16 = jnp.float32, jnp.bfloat16


def iota(shape, axis):
    return lax.broadcasted_iota(jnp.int32, shape, axis)


def column(row, rows_each):
    count = row.shape[1]
    shape = (count * rows_each, count)
    place = iota(shape, 0) // rows_each
    expert = (place % (count // 2)) * 2 + place // (count // 2)
    spread = jnp.where(iota(shape, 1) == expert, jnp.broadcast_to(row, shape), 0.0)
    return jnp.sum(spread, axis=1, keepdims=True)


def pick_kernel(picks_in, gates_in, tokens_in, cotangent_in, out, picks, gates, both, sems):
    token_rows = tokens_in.shape[0]
    copies = [
        pltpu.make_async_copy(source, target, sems.at[i])
        for i, (source, target) in enumerate(
            (
                (picks_in, picks),
                (gates_in, gates),
                (tokens_in, both.at[pl.ds(0, token_rows)]),
                (cotangent_in, both.at[pl.ds(token_rows, token_rows)]),
            )
        )
    ]
    for copy in copies:
        copy.start()
    copies[0].wait()
    copies[1].wait()
    count = picks.shape[1]
    row = column(picks[...].astype(F32), 2).astype(jnp.int32)
    gate = column(gates[...], 2)
    shape = (2 * count, 2 * token_rows)
    odd = iota((2 * count, 1), 0) % 2
    selector = (iota(shape, 1) == row + odd * token_rows).astype(F32).astype(BF16)
    copies[2].wait()
    copies[3].wait()
    picked = jnp.dot(selector, both[...], preferred_element_type=F32)
    scaled = picked * jnp.where(odd == 1, gate, 1.0)
    out[...] = scaled.reshape(out.shape).astype(BF16)


def spread_kernel(rows, weights, out):
    batches, _, count, width = out.shape
    values = rows[...].astype(F32)
    for kind in range(2):
        half = values[:, 8 * kind : 8 * kind + 8, :]
        half = half.reshape(count, width).astype(BF16)
        for i in range(batches):
            out[i, kind] = half


def sum_kernel(parts, filled, out):
    out[...] = jnp.sum(parts[...].astype(F32), 0).astype(BF16)


def scatter_kernel(picks, returned, out):
    count, token_rows = picks.shape[1], out.shape[0]
    row = column(picks[...].astype(F32), 1).astype(jnp.int32)
    selector = (iota((count, token_rows), 1) == row).astype(F32).astype(BF16)
    out[...] = tn(selector, returned[...]).astype(BF16)


def fill_kernel(core_ref, *refs):
    away = 1 - core_ref[0]
    theirs, (filled, *outs), sems = refs[:3], refs[6:10], refs[10]
    copies = [
        pltpu.make_async_copy(theirs[i].at[away], outs[i].at[away], sems.at[i]) for i in range(3)
    ]
    for copy in copies:
        copy.start()
    for copy in copies:
        copy.wait()
    filled[...] = jnp.ones_like(filled)


def nt(a, b):
    return lax.dot_general(a, b, (((1,), (1,)), ((), ())), preferred_element_type=F32)


def tn(a, b):
    return lax.dot_general(a, b, (((0,), (0,)), ((), ())), preferred_element_type=F32)


def products_kernel(got, weights, part, acts):
    batches, _, count, width = got.shape
    x = got[:, 0].reshape(batches * count, width)
    dy = got[:, 1].reshape(batches * count, width)
    for half in range(2):
        pre_gate = nt(weights[half, 0], x)
        pre_up = nt(weights[half, 1], x)
        grad_hidden = nt(weights[half, 2], dy)
        sig = jax.nn.sigmoid(pre_gate)
        active = pre_gate * sig
        acts[0, half] = (grad_hidden * pre_up * sig * (1.0 + pre_gate * (1.0 - sig))).astype(BF16)
        acts[1, half] = (grad_hidden * active).astype(BF16)
        acts[2, half] = (active * pre_up).astype(BF16)
    total = tn(acts[0, 0], weights[0, 0]) + tn(acts[1, 0], weights[0, 1])
    total += tn(acts[0, 1], weights[1, 0]) + tn(acts[1, 1], weights[1, 1])
    part[...] = total.astype(BF16).reshape(part.shape)


def grads_kernel(core_ref, acts, got, gate, up, down, *rest):
    sends, mine, sems = rest[:3], rest[3], rest[4]
    core = core_ref[0]
    rows = got.shape[0] * got.shape[2]
    stores = []
    for i, out in enumerate((gate, up, down)):
        side = got[:, i // 2].reshape(rows, got.shape[3])
        mine[i] = jnp.dot(acts[i, 0], side, preferred_element_type=F32).astype(BF16)
        stores.append(pltpu.make_async_copy(mine.at[i], out.at[core], sems.at[i]))
        stores[-1].start()
        sends[i][...] = jnp.dot(acts[i, 1], side, preferred_element_type=F32).astype(BF16)
    for copy in stores:
        copy.wait()


def shards(tokens, cotangent, picks, gates, w_gate, w_up, w_down):
    token_rows, width = tokens.shape
    count = picks.shape[1]
    units = w_gate.shape[1]
    core = lax.axis_index("core")
    small = pltpu.CompilerParams(vmem_limit_bytes=12 * 2**20)
    full = pltpu.CompilerParams(vmem_limit_bytes=63 * 2**20)
    medium = pltpu.CompilerParams(vmem_limit_bytes=20 * 2**20)
    scalar = pl.BlockSpec(memory_space=pltpu.SMEM)
    near = pl.BlockSpec(memory_space=pltpu.VMEM)
    far = pl.BlockSpec(memory_space=pl.ANY)
    place = core.reshape(1)

    def of(expert, *arrays):
        return jnp.stack(
            [lax.dynamic_index_in_dim(w, expert, 0, keepdims=False) for w in arrays]
        )

    halves = jnp.stack(
        [
            of(core, w_gate, w_up, w_down),
            jnp.concatenate(
                [
                    lax.ppermute(of(1 - core, *arrays), "core", SWAP)
                    for arrays in ((w_gate, w_up), (w_down,))
                ],
                0,
            ),
        ]
    )

    out = pl.pallas_call(
        pick_kernel,
        in_specs=[far] * 4,
        out_specs=near,
        out_shape=jax.ShapeDtypeStruct((count, 16, width // 8), BF16),
        scratch_shapes=[
            pltpu.VMEM((1, count), jnp.int32),
            pltpu.VMEM((1, count), F32),
            pltpu.VMEM((2 * token_rows, width), BF16),
            pltpu.SemaphoreType.DMA((4,)),
        ],
        compiler_params=full,
    )(picks, gates, tokens, cotangent)
    rows = lax.all_to_all(out, DEST, split_axis=0, concat_axis=0, tiled=True)
    batches = lax.axis_size(BATCH)
    sources = batches * count
    everyone = pl.pallas_call(
        spread_kernel,
        in_specs=[near, far],
        out_specs=near,
        out_shape=jax.ShapeDtypeStruct((batches, 2, count, width), BF16),
        compiler_params=small,
    )(rows, halves)
    got = lax.all_to_all(everyone, BATCH, split_axis=0, concat_axis=0, tiled=True)

    part, acts = pl.pallas_call(
        products_kernel,
        in_specs=[near] * 2,
        out_specs=[near] * 2,
        out_shape=[
            jax.ShapeDtypeStruct((batches, count, width), BF16),
            jax.ShapeDtypeStruct((3, 2, units, sources), BF16),
        ],
        cost_estimate=pl.CostEstimate(
            flops=20 * sources * units * width, bytes_accessed=8 * 2**20, transcendentals=0
        ),
        compiler_params=medium,
    )(got, halves)
    parts = lax.all_to_all(part, BATCH, split_axis=0, concat_axis=0, tiled=True)

    side = jax.ShapeDtypeStruct((units, width), BF16)
    grad = jax.ShapeDtypeStruct((2, units, width), BF16)
    results = pl.pallas_call(
        grads_kernel,
        in_specs=[scalar, near, near],
        out_specs=[far] * 3 + [near] * 3,
        out_shape=[grad] * 3 + [side] * 3,
        scratch_shapes=[pltpu.VMEM((3, units, width), BF16), pltpu.SemaphoreType.DMA((3,))],
        cost_estimate=pl.CostEstimate(
            flops=12 * sources * units * width, bytes_accessed=6 * 2**20, transcendentals=0
        ),
        compiler_params=medium,
    )(place, acts, got)
    theirs = [lax.all_gather(send, "core", axis=0) for send in results[3:]]
    filled, *grads = pl.pallas_call(
        fill_kernel,
        in_specs=[scalar] + [near] * 3 + [far] * 3,
        out_specs=[near] + [far] * 3,
        out_shape=[jax.ShapeDtypeStruct((8, 128), F32)] + [grad] * 3,
        input_output_aliases={4: 1, 5: 2, 6: 3},
        scratch_shapes=[pltpu.SemaphoreType.DMA((3,))],
        compiler_params=small,
    )(place, *theirs, *results[:3])
    summed = pl.pallas_call(
        sum_kernel,
        in_specs=[near] * 2,
        out_specs=near,
        out_shape=jax.ShapeDtypeStruct((count, width), BF16),
        compiler_params=small,
    )(parts, filled)
    returned = lax.all_to_all(
        summed.reshape(count, 2, width // 2), DEST, split_axis=0, concat_axis=0, tiled=True
    )
    grad_tokens = pl.pallas_call(
        scatter_kernel,
        in_specs=[near, near],
        out_specs=near,
        out_shape=jax.ShapeDtypeStruct((token_rows, width), BF16),
        compiler_params=small,
    )(picks, returned.reshape(count, width))
    return grad_tokens, *grads


def solution(mesh):
    fine = Mesh(mesh.devices.reshape(2, 4, 2, 2, 16), AXES)
    rows = P(AXES, None)
    weights = P(("xl", "z"), ("xh", "y", "core"), None)
    return jax.shard_map(
        shards,
        mesh=fine,
        in_specs=(rows, rows, rows, rows, weights, weights, weights),
        out_specs=(rows, weights, weights, weights),
        check_vma=False,
    )
```

```python
import jax
import jax.numpy as jnp
from jax import lax
from jax.experimental import pallas as pl
from jax.experimental.pallas import tpu as pltpu
from jax.sharding import Mesh, PartitionSpec as P

AXES = ("xh", "y", "core", "xl", "z")
DEST = ("core", "xl", "z")
BATCH = ("xh", "y")
SWAP = ((0, 1), (1, 0))
F32, BF16 = jnp.float32, jnp.bfloat16


def iota(shape, axis):
    return lax.broadcasted_iota(jnp.int32, shape, axis)


def column(row, rows_each):
    count = row.shape[1]
    shape = (count * rows_each, count)
    place = iota(shape, 0) // rows_each
    expert = (place % (count // 2)) * 2 + place // (count // 2)
    spread = jnp.where(iota(shape, 1) == expert, jnp.broadcast_to(row, shape), 0.0)
    return jnp.sum(spread, axis=1, keepdims=True)


def pick_kernel(picks_in, gates_in, tokens_in, cotangent_in, out, picks, gates, both, sems):
    token_rows = tokens_in.shape[0]
    copies = [
        pltpu.make_async_copy(source, target, sems.at[i])
        for i, (source, target) in enumerate(
            (
                (picks_in, picks),
                (gates_in, gates),
                (tokens_in, both.at[pl.ds(0, token_rows)]),
                (cotangent_in, both.at[pl.ds(token_rows, token_rows)]),
            )
        )
    ]
    for copy in copies:
        copy.start()
    copies[0].wait()
    copies[1].wait()
    count = picks.shape[1]
    row = column(picks[...].astype(F32), 2).astype(jnp.int32)
    gate = column(gates[...], 2)
    shape = (2 * count, 2 * token_rows)
    odd = iota((2 * count, 1), 0) % 2
    selector = (iota(shape, 1) == row + odd * token_rows).astype(F32).astype(BF16)
    copies[2].wait()
    copies[3].wait()
    picked = jnp.dot(selector, both[...], preferred_element_type=F32)
    scaled = picked * jnp.where(odd == 1, gate, 1.0)
    out[...] = scaled.reshape(out.shape).astype(BF16)


def spread_kernel(rows, weights, out):
    batches, _, count, width = out.shape
    values = rows[...].astype(F32)
    for kind in range(2):
        half = values[:, 8 * kind : 8 * kind + 8, :]
        half = half.reshape(count, width).astype(BF16)
        for i in range(batches):
            out[i, kind] = half


def sum_kernel(parts, filled, out):
    out[...] = jnp.sum(parts[...].astype(F32), 0).astype(BF16)


def scatter_kernel(picks, returned, out):
    count, token_rows = picks.shape[1], out.shape[0]
    row = column(picks[...].astype(F32), 1).astype(jnp.int32)
    selector = (iota((count, token_rows), 1) == row).astype(F32).astype(BF16)
    out[...] = tn(selector, returned[...]).astype(BF16)


def fill_kernel(core_ref, *refs):
    away = 1 - core_ref[0]
    theirs, (filled, *outs), sems = refs[:3], refs[6:10], refs[10]
    copies = [
        pltpu.make_async_copy(theirs[i].at[away], outs[i].at[away], sems.at[i]) for i in range(3)
    ]
    for copy in copies:
        copy.start()
    for copy in copies:
        copy.wait()
    filled[...] = jnp.ones_like(filled)


def nt(a, b):
    return lax.dot_general(a, b, (((1,), (1,)), ((), ())), preferred_element_type=F32)


def tn(a, b):
    return lax.dot_general(a, b, (((0,), (0,)), ((), ())), preferred_element_type=F32)


def products_kernel(got, weights, part, acts):
    batches, _, count, width = got.shape
    x = got[:, 0].reshape(batches * count, width)
    dy = got[:, 1].reshape(batches * count, width)
    for half in range(2):
        pre_gate = nt(weights[half, 0], x)
        pre_up = nt(weights[half, 1], x)
        grad_hidden = nt(weights[half, 2], dy)
        sig = jax.nn.sigmoid(pre_gate)
        active = pre_gate * sig
        acts[0, half] = (grad_hidden * pre_up * sig * (1.0 + pre_gate * (1.0 - sig))).astype(BF16)
        acts[1, half] = (grad_hidden * active).astype(BF16)
        acts[2, half] = (active * pre_up).astype(BF16)
    total = tn(acts[0, 0], weights[0, 0]) + tn(acts[1, 0], weights[0, 1])
    total += tn(acts[0, 1], weights[1, 0]) + tn(acts[1, 1], weights[1, 1])
    part[...] = total.astype(BF16).reshape(part.shape)


def grads_kernel(core_ref, acts, got_in, gate, up, down, *rest):
    sends, (mine, got, sems) = rest[:3], rest[3:]
    load = pltpu.make_async_copy(got_in, got, sems.at[3])
    load.start()
    load.wait()
    core = core_ref[0]
    rows = got.shape[0] * got.shape[2]
    stores = []
    for i, out in enumerate((gate, up, down)):
        side = got[:, i // 2].reshape(rows, got.shape[3])
        mine[i] = jnp.dot(acts[i, 0], side, preferred_element_type=F32).astype(BF16)
        stores.append(pltpu.make_async_copy(mine.at[i], out.at[core], sems.at[i]))
        stores[-1].start()
        sends[i][...] = jnp.dot(acts[i, 1], side, preferred_element_type=F32).astype(BF16)
    for copy in stores:
        copy.wait()


def shards(tokens, cotangent, picks, gates, w_gate, w_up, w_down):
    token_rows, width = tokens.shape
    count = picks.shape[1]
    units = w_gate.shape[1]
    core = lax.axis_index("core")
    small = pltpu.CompilerParams(vmem_limit_bytes=12 * 2**20)
    full = pltpu.CompilerParams(vmem_limit_bytes=63 * 2**20)
    medium = pltpu.CompilerParams(vmem_limit_bytes=20 * 2**20)
    scalar = pl.BlockSpec(memory_space=pltpu.SMEM)
    near = pl.BlockSpec(memory_space=pltpu.VMEM)
    far = pl.BlockSpec(memory_space=pl.ANY)
    place = core.reshape(1)

    def of(expert, *arrays):
        return jnp.stack(
            [lax.dynamic_index_in_dim(w, expert, 0, keepdims=False) for w in arrays]
        )

    halves = jnp.stack(
        [
            of(core, w_gate, w_up, w_down),
            jnp.concatenate(
                [
                    lax.ppermute(of(1 - core, *arrays), "core", SWAP)
                    for arrays in ((w_gate, w_up), (w_down,))
                ],
                0,
            ),
        ]
    )

    out = pl.pallas_call(
        pick_kernel,
        in_specs=[far] * 4,
        out_specs=near,
        out_shape=jax.ShapeDtypeStruct((count, 16, width // 8), BF16),
        scratch_shapes=[
            pltpu.VMEM((1, count), jnp.int32),
            pltpu.VMEM((1, count), F32),
            pltpu.VMEM((2 * token_rows, width), BF16),
            pltpu.SemaphoreType.DMA((4,)),
        ],
        compiler_params=full,
    )(picks, gates, tokens, cotangent)
    rows = lax.all_to_all(out, DEST, split_axis=0, concat_axis=0, tiled=True)
    batches = lax.axis_size(BATCH)
    sources = batches * count
    everyone = pl.pallas_call(
        spread_kernel,
        in_specs=[near, far],
        out_specs=near,
        out_shape=jax.ShapeDtypeStruct((batches, 2, count, width), BF16),
        compiler_params=small,
    )(rows, halves)
    got = lax.all_to_all(everyone, BATCH, split_axis=0, concat_axis=0, tiled=True)

    part, acts = pl.pallas_call(
        products_kernel,
        in_specs=[near] * 2,
        out_specs=[near] * 2,
        out_shape=[
            jax.ShapeDtypeStruct((batches, count, width), BF16),
            jax.ShapeDtypeStruct((3, 2, units, sources), BF16),
        ],
        cost_estimate=pl.CostEstimate(
            flops=20 * sources * units * width, bytes_accessed=8 * 2**20, transcendentals=0
        ),
        compiler_params=medium,
    )(got, halves)
    parts = lax.all_to_all(part, BATCH, split_axis=0, concat_axis=0, tiled=True)

    side = jax.ShapeDtypeStruct((units, width), BF16)
    grad = jax.ShapeDtypeStruct((2, units, width), BF16)
    results = pl.pallas_call(
        grads_kernel,
        in_specs=[scalar, near, far],
        out_specs=[far] * 3 + [near] * 3,
        out_shape=[grad] * 3 + [side] * 3,
        scratch_shapes=[
            pltpu.VMEM((3, units, width), BF16),
            pltpu.VMEM(got.shape, BF16),
            pltpu.SemaphoreType.DMA((4,)),
        ],
        cost_estimate=pl.CostEstimate(
            flops=12 * sources * units * width, bytes_accessed=6 * 2**20, transcendentals=0
        ),
        compiler_params=pltpu.CompilerParams(vmem_limit_bytes=60000000),
    )(place, acts, got)
    theirs = [lax.all_gather(send, "core", axis=0) for send in results[3:]]
    filled, *grads = pl.pallas_call(
        fill_kernel,
        in_specs=[scalar] + [near] * 3 + [far] * 3,
        out_specs=[near] + [far] * 3,
        out_shape=[jax.ShapeDtypeStruct((8, 128), F32)] + [grad] * 3,
        input_output_aliases={4: 1, 5: 2, 6: 3},
        scratch_shapes=[pltpu.SemaphoreType.DMA((3,))],
        compiler_params=small,
    )(place, *theirs, *results[:3])
    summed = pl.pallas_call(
        sum_kernel,
        in_specs=[near] * 2,
        out_specs=near,
        out_shape=jax.ShapeDtypeStruct((count, width), BF16),
        compiler_params=small,
    )(parts, filled)
    returned = lax.all_to_all(
        summed.reshape(count, 2, width // 2), DEST, split_axis=0, concat_axis=0, tiled=True
    )
    grad_tokens = pl.pallas_call(
        scatter_kernel,
        in_specs=[near, near],
        out_specs=near,
        out_shape=jax.ShapeDtypeStruct((token_rows, width), BF16),
        compiler_params=small,
    )(picks, returned.reshape(count, width))
    return grad_tokens, *grads


def solution(mesh):
    fine = Mesh(mesh.devices.reshape(2, 4, 2, 2, 16), AXES)
    rows = P(AXES, None)
    weights = P(("xl", "z"), ("xh", "y", "core"), None)
    return jax.shard_map(
        shards,
        mesh=fine,
        in_specs=(rows, rows, rows, rows, weights, weights, weights),
        out_specs=(rows, weights, weights, weights),
        check_vma=False,
    )
```
